768 devices in a mesh: east: 96 (over z, y), north: 4 (over x), layer: 2 (over core).
Axes of the slice: x: 4, y: 8, z: 12, core: 2. Of those that a mesh axis runs over, the one named last changes fastest.
Arguments:
- recharge: float32 [8, 3072, 1024], P('layer', 'east', 'north'), may hold values from -16 to 16
- conductivity: float32 [8, 3072, 1024], P('layer', 'east', 'north'), may hold values from 0.1 to 10
- storage: float32 [8, 3072, 1024], P('layer', 'east', 'north'), may hold values from 0.1 to 1
Outputs:
- pressure: float32 [8, 3072, 1024], P('layer', 'east', 'north')
- residual: float32 [8, 3072, 1024], P('layer', 'east', 'north')
The draws below stay inside these ranges and needn't reach their ends.
All inputs are finite; a program needn't handle non-finite values.
Results may differ from the reference program's by a relative error of at most 0.039.
Values sent between devices are 32-bit elements; how exact they have to be, the bound alone decides.
No kernel may reach another device: no remote copies, remote signals or barrier semaphores. Data moves between devices by JAX's collectives and lax.ppermute only.
A program may use at most 32 MiB of HBM per device.

```python
import math
import jax
import jax.numpy as jnp

ITERS = 2
NL = 8
NE = 3072
NN = 1024


def draw_recharge(key, part):
    key = jax.random.fold_in(key, 11)
    keys = jax.random.split(key, 2)
    two_pi = 2.0 * math.pi
    lay_pos = ((jnp.arange(NL, dtype=jnp.float32) + 0.5) / NL)[:, None, None]
    east_pos = ((jnp.arange(NE, dtype=jnp.float32) + 0.5) / NE)[None, :, None]
    north_pos = ((jnp.arange(NN, dtype=jnp.float32) + 0.5) / NN)[None, None, :]
    phases = jax.random.uniform(keys[0], (4,), jnp.float32, 0.0, two_pi)
    envelope = jnp.exp(1.2 * jnp.cos(two_pi * (east_pos + 0.5 * north_pos) + phases[0]))
    first_mode = jnp.cos(two_pi * (east_pos + north_pos) + phases[1])
    second_mode = jnp.cos(two_pi * (2.0 * east_pos - north_pos + 0.5 * lay_pos) + phases[2])
    third_mode = jnp.cos(two_pi * (3.0 * east_pos + 2.0 * north_pos) + phases[3])
    rough = jnp.clip(jax.random.normal(keys[1], (NL, NE, NN), jnp.float32), -4.0, 4.0)
    smooth = first_mode + 0.7 * second_mode + 0.5 * third_mode
    return (rough * envelope + smooth).astype(jnp.float32)


def block_levels(key, dims, pieces, least, largest):
    factor_of, own = 1.0, jax.random.fold_in(key, 6)
    for dim, parts in pieces:
        steps = jnp.exp(jax.random.uniform(jax.random.fold_in(own, dim), (parts,), jnp.float32, least / len(pieces), largest / len(pieces)))
        factor_of = factor_of * jnp.repeat(steps, dims[dim] // parts).reshape([-1 if axis == dim else 1 for axis in range(len(dims))])
    return factor_of


def setup_inputs(seed: int = 0) -> dict:
    arg_keys = jax.random.split(jax.random.key(seed), 4)
    return {
        "recharge": draw_recharge(jax.random.fold_in(arg_keys[3], 71), 0),
        "conductivity": jnp.clip(jnp.exp(math.log(10.0) - 4.6051702 * jax.random.uniform(arg_keys[1], (NL, NE, NN), jnp.float32) ** block_levels(arg_keys[1], (NL, NE, NN), ((0, 2), (1, 96), (2, 4)), -0.2, 0.2)), 0.1, 10.0),
        "storage": jnp.clip(jnp.exp(math.log(1.0) - 2.3025851 * jax.random.uniform(arg_keys[2], (NL, NE, NN), jnp.float32) ** block_levels(arg_keys[2], (NL, NE, NN), ((0, 2), (1, 96), (2, 4)), -0.2, 0.2)), 0.1, 1.0),
    }


def harmonic(first, second):
    return 2.0 * first * second / (first + second)


def coefficients(conductivity, padded):
    core = conductivity
    return (
        4.0 * harmonic(core, padded[2:, 1:-1, 1:-1]),
        4.0 * harmonic(core, padded[:-2, 1:-1, 1:-1]),
        harmonic(core, padded[1:-1, 2:, 1:-1]),
        harmonic(core, padded[1:-1, :-2, 1:-1]),
        harmonic(core, padded[1:-1, 1:-1, 2:]),
        harmonic(core, padded[1:-1, 1:-1, :-2]),
    )


def apply_operator(field, padded, faces, diag):
    beside = faces[0] * padded[2:, 1:-1, 1:-1] + faces[1] * padded[:-2, 1:-1, 1:-1]
    beside = beside + faces[2] * padded[1:-1, 2:, 1:-1] + faces[3] * padded[1:-1, :-2, 1:-1]
    beside = beside + faces[4] * padded[1:-1, 1:-1, 2:] + faces[5] * padded[1:-1, 1:-1, :-2]
    return diag * field - beside


def reference(recharge, conductivity, storage):
    faces = coefficients(conductivity, jnp.pad(conductivity, 1))
    diag = storage + faces[0] + faces[1] + faces[2] + faces[3] + faces[4] + faces[5]
    pressure = jnp.zeros_like(recharge)
    residual = recharge
    precond = residual / diag
    direction = precond
    rz_now = jnp.sum(residual * precond)
    for step in range(ITERS):
        image = apply_operator(direction, jnp.pad(direction, 1), faces, diag)
        alpha = rz_now / jnp.sum(direction * image)
        pressure = pressure + alpha * direction
        residual = residual - alpha * image
        if step + 1 < ITERS:
            precond = residual / diag
            rz_next = jnp.sum(residual * precond)
            direction = precond + (rz_next / rz_now) * direction
            rz_now = rz_next
    return pressure, residual
```

```python
import jax
import jax.numpy as jnp
from jax import lax
from jax.experimental import pallas as pl
from jax.experimental.pallas import tpu as pltpu
from jax.sharding import Mesh, PartitionSpec as P

EAST = ("z", "y")
ALL = ("z", "y", "x", "c")
F32 = jnp.float32

NK, NR = 7, 6
SLABS = NK + 2 * NR
SIDE = [("k", j) for j in range(6)] + [("r", j) for j in range(5)] + [("s", j) for j in range(5)]
SIDE_AT = {name: i for i, name in enumerate(SIDE)}


def slab_index(name, j):
    return {"k": 0, "r": NK, "s": NK + NR}[name] + j


def pack_layer(r_ref, k_ref, s_ref, own_ref, out_ref):
    core = lax.axis_index("c")
    at = 0
    for base, ref, count in ((0, k_ref, 3), (4, r_ref, 2), (8, s_ref, 2)):
        for j in range(4):
            own_ref[base + j] = ref[jnp.where(core == 0, j, 3 - j)]
        for j in range(count):
            out_ref[at] = ref[jnp.where(core == 0, 3 - j, j)]
            at += 1


def main_slab(own_ref, in_ref, name, j):
    base, beside = {"k": (0, 0), "r": (4, 3), "s": (8, 5)}[name]
    return own_ref[base + j] if j < 4 else in_ref[beside + j - 4]


def pack_north(own_ref, in_ref, low_ref, high_ref):
    lane = lax.broadcasted_iota(jnp.int32, (32, 128), 1)
    low = jnp.zeros((32, 128), F32)
    high = jnp.zeros((32, 128), F32)
    for i, (name, j) in enumerate(SIDE):
        slab = main_slab(own_ref, in_ref, name, j)
        mine = (lane >= 3 * i) & (lane < 3 * i + 3)
        low = jnp.where(mine, pltpu.roll(slab[:, :128], 3 * i, 1) if i else slab[:, :128], low)
        high = jnp.where(mine, pltpu.roll(slab[:, 128:], 3 * i + 3, 1), high)
    low_ref[...] = low
    high_ref[...] = high


def pack_east(own_ref, in_ref, from_low_ref, from_high_ref, wide_ref, low_ref, high_ref):
    lane = lax.broadcasted_iota(jnp.int32, (32, 128), 1)
    from_low, from_high = from_low_ref[...], from_high_ref[...]
    for name, count in (("k", NK), ("r", NR), ("s", NR)):
        for j in range(count):
            at = slab_index(name, j)
            wide_ref[at, :, :256] = main_slab(own_ref, in_ref, name, j)
            beyond = jnp.zeros((32, 128), F32)
            if (name, j) in SIDE_AT:
                i = SIDE_AT[name, j]
                above = pltpu.roll(from_high, 128 - 3 * i, 1) if i else from_high
                below = pltpu.roll(from_low, 125 - 3 * i, 1)
                beyond = jnp.where(lane < 3, above, jnp.where(lane >= 125, below, 0.0))
            wide_ref[at, :, 256:] = beyond
    row = lax.broadcasted_iota(jnp.int32, (8, 384), 0)
    for j in range(6):
        low, high = wide_ref[j, 0:8, :], wide_ref[j, 24:32, :]
        if j < 5:
            r, s = slab_index("r", j), slab_index("s", j)
            low = jnp.where(row < 3, low, jnp.where(row < 5, pltpu.roll(wide_ref[r, 0:8, :], 3, 0), pltpu.roll(wide_ref[s, 0:8, :], 5, 0)))
            high = jnp.where(row >= 5, high, jnp.where(row >= 3, pltpu.roll(wide_ref[r, 24:32, :], 5, 0), pltpu.roll(wide_ref[s, 24:32, :], 3, 0)))
        low_ref[j] = low
        high_ref[j] = high


def harmonic(first, second):
    return 2.0 * first * second / jnp.maximum(first + second, 1e-30)


def operate(wide_ref, from_low_ref, from_high_ref, z_ref, q_ref, w_ref, u_ref, sums_ref):
    row = lax.broadcasted_iota(jnp.int32, (8, 384), 0)

    def whole(name, j):
        main = wide_ref[slab_index(name, j)]
        if (name, j) not in SIDE_AT:
            beyond = jnp.zeros((8, 384), F32)
        else:
            above, below = from_high_ref[j], from_low_ref[j]
            if name == "k":
                beyond = jnp.where(row < 3, above, jnp.where(row >= 5, below, 0.0))
            else:
                up, down = (5, 3) if name == "r" else (3, 5)
                beyond = jnp.where(row < 2, pltpu.roll(above, up, 0), jnp.where(row >= 6, pltpu.roll(below, down, 0), 0.0))
        return jnp.concatenate([main, beyond], axis=0)

    def north(v):
        return pltpu.roll(v, 383, 1)

    def south(v):
        return pltpu.roll(v, 1, 1)

    def east(v):
        return pltpu.roll(v, 39, 0)

    def west(v):
        return pltpu.roll(v, 1, 0)

    k = [whole("k", j) for j in range(NK)]
    face_l = [4.0 * harmonic(k[j], k[j + 1]) for j in range(NR)]
    face_e = [harmonic(k[j], east(k[j])) for j in range(NR)]
    face_n = [harmonic(k[j], north(k[j])) for j in range(NR)]
    diag, z = [], []
    for j in range(NR):
        d = whole("s", j) + face_l[j] + face_e[j] + west(face_e[j]) + face_n[j] + south(face_n[j])
        if j:
            d = d + face_l[j - 1]
        d = jnp.where(d > 0.0, d, 1.0)
        diag.append(d)
        z.append(whole("r", j) / d)

    def apply(v, count):
        out = []
        for j in range(count):
            beside = face_l[j] * v[j + 1] + face_e[j] * east(v[j]) + west(face_e[j] * v[j])
            beside = beside + face_n[j] * north(v[j]) + south(face_n[j] * v[j])
            if j:
                beside = beside + face_l[j - 1] * v[j - 1]
            out.append(diag[j] * v[j] - beside)
        return out

    q = apply(z, 5)
    w = [q[j] / diag[j] for j in range(5)]
    u = apply(w, 4)
    totals = [jnp.zeros((8, 128), F32)] * 4
    for j in range(4):
        own = [v[j][:32, :256] for v in (z, q, w, u)]
        for ref, v in zip((z_ref, q_ref, w_ref, u_ref), own):
            ref[j] = v
        zo, qo, wo, uo = own
        rz = wide_ref[slab_index("r", j), :, :256] * zo
        for i, product in enumerate((rz, zo * qo, qo * wo, wo * uo)):
            for a in range(4):
                for b in range(2):
                    totals[i] = totals[i] + product[8 * a : 8 * a + 8, 128 * b : 128 * b + 128]
    lane = lax.broadcasted_iota(jnp.int32, (1, 128), 1)
    line = jnp.zeros((1, 128), F32)
    for i in range(4):
        line = jnp.where(lane == i, jnp.sum(totals[i]), line)
    for i in range(sums_ref.shape[0]):
        sums_ref[i] = line


def finish(sums_ref, r_ref, z_ref, q_ref, w_ref, u_ref, pressure_ref, residual_ref):
    core = lax.axis_index("c")
    line = sums_ref[0]
    for i in range(1, sums_ref.shape[0]):
        line = line + sums_ref[i]
    lane = lax.broadcasted_iota(jnp.int32, (1, 128), 1)
    rz, zq, qw, wu = (jnp.sum(jnp.where(lane == i, line, 0.0), axis=1, keepdims=True) for i in range(4))
    alpha = rz / zq
    rz_next = alpha * alpha * qw - rz
    grown = 1.0 + rz_next / rz
    curve = grown * grown * zq - 2.0 * grown * alpha * qw + alpha * alpha * wu
    alpha_next = rz_next / curve
    along = alpha + alpha_next * grown
    across = alpha * alpha_next
    for j in range(4):
        to = jnp.where(core == 0, j, 3 - j)
        pressure_ref[to] = along * z_ref[j] - across * w_ref[j]
        residual_ref[to] = r_ref[4 + j] - along * q_ref[j] + across * u_ref[j]


def call(kernel, *shapes):
    in_vmem = pl.BlockSpec(memory_space=pltpu.VMEM)

    def run(*args):
        return pl.pallas_call(
            kernel,
            out_shape=[jax.ShapeDtypeStruct(shape, F32) for shape in shapes],
            in_specs=[in_vmem] * len(args),
            out_specs=[in_vmem] * len(shapes),
            compiler_params=pltpu.CompilerParams(vmem_limit_bytes=32 * 1024 * 1024),
        )(*args)

    return run


def chain(count):
    up = [(i, i + 1) for i in range(count - 1)]
    return up, [(target, source) for source, target in up]


def spread_sum(line, axes, count):
    return lax.all_to_all(jnp.broadcast_to(line[None], (count, 1, 128)), axes, 0, 0)


def per_device(recharge, conductivity, storage):
    size = {axis: lax.axis_size(axis) for axis in ALL}
    own, out = call(pack_layer, (12, 32, 256), (7, 32, 256))(recharge, conductivity, storage)
    beside = lax.ppermute(out, "c", [(0, 1), (1, 0)])
    low, high = call(pack_north, (32, 128), (32, 128))(own, beside)
    up, down = chain(size["x"])
    from_low, from_high = lax.ppermute(high, "x", up), lax.ppermute(low, "x", down)
    wide, low, high = call(pack_east, (SLABS, 32, 384), (6, 8, 384), (6, 8, 384))(own, beside, from_low, from_high)
    up, down = chain(size["z"] * size["y"])
    from_low, from_high = lax.ppermute(high, EAST, up), lax.ppermute(low, EAST, down)
    first = size["y"] * size["x"]
    block = (4, 32, 256)
    z, q, w, u, sums = call(operate, block, block, block, block, (first, 1, 128))(wide, from_low, from_high)
    sums = lax.all_to_all(sums, ("y", "x"), 0, 0)
    sums = spread_sum(jnp.sum(sums, axis=0), ("z", "c"), size["z"] * size["c"])
    return tuple(call(finish, block, block)(sums, own, z, q, w, u))


def solution(mesh):
    east, north, layer = (mesh.shape[axis] for axis in ("east", "north", "layer"))
    row = 8 if east % 8 == 0 else 1
    fine = Mesh(mesh.devices.reshape(east // row, row, north, layer), ALL)
    placed = P("c", EAST, "x")
    return jax.shard_map(
        per_device, mesh=fine, in_specs=(placed,) * 3, out_specs=(placed,) * 2, check_vma=False
    )
```

```python
import functools

import jax
import jax.numpy as jnp
from jax import lax
from jax.experimental import pallas as pl
from jax.experimental.pallas import tpu as pltpu
from jax.sharding import Mesh, PartitionSpec as P

EAST = ("z", "y")
ALL = ("z", "y", "x", "c")
F32 = jnp.float32

NK, NR = 7, 6
SLABS = NK + 2 * NR
SIDE = [("k", j) for j in range(6)] + [("r", j) for j in range(5)] + [("s", j) for j in range(5)]
OWN = {"k": 0, "r": 4, "s": 8}
HALF = 64


def slab_index(name, j):
    return {"k": 0, "r": NK, "s": NK + NR}[name] + j


def pack_own(r_hbm, k_hbm, s_hbm, own_ref, out_ref, side_ref, r_ref, k_ref, s_ref, arrived):
    copies = [
        pltpu.make_async_copy(source, target, arrived.at[i])
        for i, (source, target) in enumerate(((k_hbm, k_ref), (r_hbm, r_ref), (s_hbm, s_ref)))
    ]
    for copy in copies:
        copy.start()
    core = lax.axis_index("c")
    lane = lax.broadcasted_iota(jnp.int32, (32, 128), 1)
    line = jnp.zeros((32, 128), F32)
    at = 0
    for copy, ref, name, count in zip(copies, (k_ref, r_ref, s_ref), "krs", (3, 2, 2)):
        copy.wait()
        for j in range(4):
            slab = ref[jnp.where(core == 0, j, 3 - j)]
            i = OWN[name] + j
            own_ref[i] = slab
            low, high = slab[:, :128], pltpu.roll(slab[:, 128:], 3 * i + HALF + 3, 1)
            low = pltpu.roll(low, 3 * i, 1) if i else low
            line = jnp.where((lane >= 3 * i) & (lane < 3 * i + 3), low, line)
            line = jnp.where((lane >= HALF + 3 * i) & (lane < HALF + 3 * i + 3), high, line)
        for j in range(count):
            out_ref[at] = ref[jnp.where(core == 0, 3 - j, j)]
            at += 1
    for i in range(side_ref.shape[0]):
        side_ref[i] = line


def main_slab(own_ref, in_ref, name, j):
    beside = {"k": 0, "r": 3, "s": 5}[name]
    return own_ref[OWN[name] + j] if j < 4 else in_ref[beside + j - 4]


def pack_east(north_count, own_ref, in_ref, side_ref, wide_ref, low_ref, high_ref):
    lane = lax.broadcasted_iota(jnp.int32, (32, 128), 1)
    core, place = lax.axis_index("c"), lax.axis_index("x")
    up, down = jnp.minimum(place + 1, north_count - 1), jnp.maximum(place - 1, 0)
    has_up, has_down = place < north_count - 1, place > 0
    same = (side_ref[2 * up + core], side_ref[2 * down + core])
    other = (side_ref[2 * up + 1 - core], side_ref[2 * down + 1 - core])
    take_up, take_down = (lane < 3) & has_up, (lane >= 125) & has_down
    for name, count in (("k", NK), ("r", NR), ("s", NR)):
        for j in range(count):
            at = slab_index(name, j)
            wide_ref[at, :, :256] = main_slab(own_ref, in_ref, name, j)
            beyond = jnp.zeros((32, 128), F32)
            if (name, j) in SIDE:
                above, below = same if j < 4 else other
                i = OWN[name] + (j if j < 4 else 7 - j)
                above = pltpu.roll(above, 128 - 3 * i, 1) if i else above
                below = pltpu.roll(below, (125 - HALF - 3 * i) % 128, 1)
                beyond = jnp.where(take_up, above, jnp.where(take_down, below, 0.0))
            wide_ref[at, :, 256:] = beyond
    row = lax.broadcasted_iota(jnp.int32, (8, 384), 0)
    for j in range(6):
        low, high = wide_ref[j, 0:8, :], wide_ref[j, 24:32, :]
        if j < 5:
            r, s = slab_index("r", j), slab_index("s", j)
            low = jnp.where(row < 3, low, jnp.where(row < 5, pltpu.roll(wide_ref[r, 0:8, :], 3, 0), pltpu.roll(wide_ref[s, 0:8, :], 5, 0)))
            high = jnp.where(row >= 5, high, jnp.where(row >= 3, pltpu.roll(wide_ref[r, 24:32, :], 5, 0), pltpu.roll(wide_ref[s, 24:32, :], 3, 0)))
        low_ref[j] = low
        high_ref[j] = high


def harmonic(first, second):
    return 2.0 * first * second / jnp.maximum(first + second, 1e-30)


def operate(wide_ref, from_low_ref, from_high_ref, z_ref, q_ref, w_ref, u_ref, sums_ref):
    row = lax.broadcasted_iota(jnp.int32, (8, 384), 0)

    def whole(name, j):
        main = wide_ref[slab_index(name, j)]
        if (name, j) not in SIDE:
            beyond = jnp.zeros((8, 384), F32)
        else:
            above, below = from_high_ref[j], from_low_ref[j]
            if name == "k":
                beyond = jnp.where(row < 3, above, jnp.where(row >= 5, below, 0.0))
            else:
                up, down = (5, 3) if name == "r" else (3, 5)
                beyond = jnp.where(row < 2, pltpu.roll(above, up, 0), jnp.where(row >= 6, pltpu.roll(below, down, 0), 0.0))
        return jnp.concatenate([main, beyond], axis=0)

    def north(v):
        return pltpu.roll(v, 383, 1)

    def south(v):
        return pltpu.roll(v, 1, 1)

    def east(v):
        return pltpu.roll(v, 39, 0)

    def west(v):
        return pltpu.roll(v, 1, 0)

    k = [whole("k", j) for j in range(NK)]
    face_l = [4.0 * harmonic(k[j], k[j + 1]) for j in range(NR)]
    face_e = [harmonic(k[j], east(k[j])) for j in range(NR)]
    face_n = [harmonic(k[j], north(k[j])) for j in range(NR)]
    diag, z = [], []
    for j in range(NR):
        d = whole("s", j) + face_l[j] + face_e[j] + west(face_e[j]) + face_n[j] + south(face_n[j])
        if j:
            d = d + face_l[j - 1]
        d = jnp.where(d > 0.0, d, 1.0)
        diag.append(d)
        z.append(whole("r", j) / d)

    def apply(v, count):
        out = []
        for j in range(count):
            beside = face_l[j] * v[j + 1] + face_e[j] * east(v[j]) + west(face_e[j] * v[j])
            beside = beside + face_n[j] * north(v[j]) + south(face_n[j] * v[j])
            if j:
                beside = beside + face_l[j - 1] * v[j - 1]
            out.append(diag[j] * v[j] - beside)
        return out

    q = apply(z, 5)
    w = [q[j] / diag[j] for j in range(5)]
    u = apply(w, 4)
    totals = [jnp.zeros((8, 128), F32)] * 4
    for j in range(4):
        own = [v[j][:32, :256] for v in (z, q, w, u)]
        for ref, v in zip((z_ref, q_ref, w_ref, u_ref), own):
            ref[j] = v
        zo, qo, wo, uo = own
        rz = wide_ref[slab_index("r", j), :, :256] * zo
        for i, product in enumerate((rz, zo * qo, qo * wo, wo * uo)):
            for a in range(4):
                for b in range(2):
                    totals[i] = totals[i] + product[8 * a : 8 * a + 8, 128 * b : 128 * b + 128]
    lane = lax.broadcasted_iota(jnp.int32, (1, 128), 1)
    line = jnp.zeros((1, 128), F32)
    for i in range(4):
        line = jnp.where(lane == i, jnp.sum(totals[i]), line)
    for i in range(sums_ref.shape[0]):
        sums_ref[i] = line


def finish(sums_ref, r_ref, z_ref, q_ref, w_ref, u_ref, pressure_ref, residual_ref):
    core = lax.axis_index("c")
    line = sums_ref[0]
    for i in range(1, sums_ref.shape[0]):
        line = line + sums_ref[i]
    lane = lax.broadcasted_iota(jnp.int32, (1, 128), 1)
    rz, zq, qw, wu = (jnp.sum(jnp.where(lane == i, line, 0.0), axis=1, keepdims=True) for i in range(4))
    alpha = rz / zq
    rz_next = alpha * alpha * qw - rz
    grown = 1.0 + rz_next / rz
    curve = grown * grown * zq - 2.0 * grown * alpha * qw + alpha * alpha * wu
    alpha_next = rz_next / curve
    along = alpha + alpha_next * grown
    across = alpha * alpha_next
    for j in range(4):
        to = jnp.where(core == 0, j, 3 - j)
        pressure_ref[to] = along * z_ref[j] - across * w_ref[j]
        residual_ref[to] = r_ref[4 + j] - along * q_ref[j] + across * u_ref[j]


def call(kernel, *shapes, space=pltpu.VMEM, scratch=(), limit=32 * 1024 * 1024):
    def run(*args):
        return pl.pallas_call(
            kernel,
            out_shape=[jax.ShapeDtypeStruct(shape, F32) for shape in shapes],
            in_specs=[pl.BlockSpec(memory_space=space)] * len(args),
            out_specs=[pl.BlockSpec(memory_space=pltpu.VMEM)] * len(shapes),
            scratch_shapes=scratch,
            compiler_params=pltpu.CompilerParams(vmem_limit_bytes=limit),
        )(*args)

    return run


def chain(count):
    up = [(i, i + 1) for i in range(count - 1)]
    return up, [(target, source) for source, target in up]


def spread_sum(line, axes, count):
    return lax.all_to_all(jnp.broadcast_to(line[None], (count, 1, 128)), axes, 0, 0)


def per_device(recharge, conductivity, storage):
    size = {axis: lax.axis_size(axis) for axis in ALL}
    block = (4, 32, 256)
    scratch = [pltpu.VMEM(block, F32)] * 3 + [pltpu.SemaphoreType.DMA((3,))]
    near = size["x"] * size["c"]
    own, out, side = call(
        pack_own, (12, 32, 256), (7, 32, 256), (near, 32, 128), space=pltpu.HBM, scratch=scratch
    )(*(pltpu.with_memory_space_constraint(v, pltpu.HBM) for v in (recharge, conductivity, storage)))
    beside = lax.ppermute(out, "c", [(0, 1), (1, 0)])
    side = lax.all_to_all(side, ("x", "c"), 0, 0)
    pack = functools.partial(pack_east, size["x"])
    wide, low, high = call(pack, (SLABS, 32, 384), (6, 8, 384), (6, 8, 384))(own, beside, side)
    up, down = chain(size["z"] * size["y"])
    from_low, from_high = lax.ppermute(high, EAST, up), lax.ppermute(low, EAST, down)
    first = size["y"] * size["x"]
    z, q, w, u, sums = call(operate, block, block, block, block, (first, 1, 128))(wide, from_low, from_high)
    sums = lax.all_to_all(sums, ("y", "x"), 0, 0)
    sums = spread_sum(jnp.sum(sums, axis=0), ("z", "c"), size["z"] * size["c"])
    return tuple(call(finish, block, block)(sums, own, z, q, w, u))


def solution(mesh):
    east, north, layer = (mesh.shape[axis] for axis in ("east", "north", "layer"))
    row = 8 if east % 8 == 0 else 1
    fine = Mesh(mesh.devices.reshape(east // row, row, north, layer), ALL)
    placed = P("c", EAST, "x")
    return jax.shard_map(
        per_device, mesh=fine, in_specs=(placed,) * 3, out_specs=(placed,) * 2, check_vma=False
    )
```

```python
import functools
import math

import jax
import jax.numpy as jnp
import numpy as np
from jax import lax
from jax.experimental import pallas as pl
from jax.experimental.pallas import tpu as pltpu
from jax.sharding import Mesh, PartitionSpec as P

EAST = ("z", "y")
ALL = ("z", "y", "x", "c")
F32 = jnp.float32

NK, NR = 7, 6
SLABS = NK + 2 * NR
SIDE = [("k", j) for j in range(6)] + [("r", j) for j in range(5)] + [("s", j) for j in range(5)]
OWN = {"k": 0, "r": 4, "s": 8}
HALF = 64


def slab_index(name, j):
    return {"k": 0, "r": NK, "s": NK + NR}[name] + j


def pack_own(r_hbm, k_hbm, s_hbm, own_ref, out_ref, side_ref, r_ref, k_ref, s_ref, arrived):
    copies = [
        pltpu.make_async_copy(source, target, arrived.at[i])
        for i, (source, target) in enumerate(((k_hbm, k_ref), (r_hbm, r_ref), (s_hbm, s_ref)))
    ]
    for copy in copies:
        copy.start()
    core = lax.axis_index("c")
    lane = lax.broadcasted_iota(jnp.int32, (32, 128), 1)
    line = jnp.zeros((32, 128), F32)
    at = 0
    for copy, ref, name, count in zip(copies, (k_ref, r_ref, s_ref), "krs", (3, 2, 2)):
        copy.wait()
        for j in range(4):
            slab = ref[jnp.where(core == 0, j, 3 - j)]
            i = OWN[name] + j
            own_ref[i] = slab
            low, high = slab[:, :128], pltpu.roll(slab[:, 128:], 3 * i + HALF + 3, 1)
            low = pltpu.roll(low, 3 * i, 1) if i else low
            line = jnp.where((lane >= 3 * i) & (lane < 3 * i + 3), low, line)
            line = jnp.where((lane >= HALF + 3 * i) & (lane < HALF + 3 * i + 3), high, line)
        for j in range(count):
            out_ref[at] = ref[jnp.where(core == 0, 3 - j, j)]
            at += 1
    for i in range(side_ref.shape[0]):
        side_ref[i] = line


def main_slab(own_ref, in_ref, name, j):
    beside = {"k": 0, "r": 3, "s": 5}[name]
    return own_ref[OWN[name] + j] if j < 4 else in_ref[beside + j - 4]


def pack_east(north_count, own_ref, in_ref, side_ref, wide_ref, low_ref, high_ref):
    lane = lax.broadcasted_iota(jnp.int32, (32, 128), 1)
    core, place = lax.axis_index("c"), lax.axis_index("x")
    up, down = jnp.minimum(place + 1, north_count - 1), jnp.maximum(place - 1, 0)
    has_up, has_down = place < north_count - 1, place > 0
    same = (side_ref[2 * up + core], side_ref[2 * down + core])
    other = (side_ref[2 * up + 1 - core], side_ref[2 * down + 1 - core])
    take_up, take_down = (lane < 3) & has_up, (lane >= 125) & has_down
    for name, count in (("k", NK), ("r", NR), ("s", NR)):
        for j in range(count):
            at = slab_index(name, j)
            wide_ref[at, :, :256] = main_slab(own_ref, in_ref, name, j)
            beyond = jnp.zeros((32, 128), F32)
            if (name, j) in SIDE:
                above, below = same if j < 4 else other
                i = OWN[name] + (j if j < 4 else 7 - j)
                above = pltpu.roll(above, 128 - 3 * i, 1) if i else above
                below = pltpu.roll(below, (125 - HALF - 3 * i) % 128, 1)
                beyond = jnp.where(take_up, above, jnp.where(take_down, below, 0.0))
            wide_ref[at, :, 256:] = beyond
    row = lax.broadcasted_iota(jnp.int32, (8, 384), 0)
    for j in range(6):
        low, high = wide_ref[j, 0:8, :], wide_ref[j, 24:32, :]
        if j < 5:
            r, s = slab_index("r", j), slab_index("s", j)
            low = jnp.where(row < 3, low, jnp.where(row < 5, pltpu.roll(wide_ref[r, 0:8, :], 3, 0), pltpu.roll(wide_ref[s, 0:8, :], 5, 0)))
            high = jnp.where(row >= 5, high, jnp.where(row >= 3, pltpu.roll(wide_ref[r, 24:32, :], 5, 0), pltpu.roll(wide_ref[s, 24:32, :], 3, 0)))
        low_ref[j] = low
        high_ref[j] = high


def harmonic(first, second):
    return 2.0 * first * second / jnp.maximum(first + second, 1e-30)


def operate(wide_ref, from_low_ref, from_high_ref, z_ref, q_ref, w_ref, u_ref, sums_ref):
    row = lax.broadcasted_iota(jnp.int32, (8, 384), 0)

    def whole(name, j):
        main = wide_ref[slab_index(name, j)]
        if (name, j) not in SIDE:
            beyond = jnp.zeros((8, 384), F32)
        else:
            above, below = from_high_ref[j], from_low_ref[j]
            if name == "k":
                beyond = jnp.where(row < 3, above, jnp.where(row >= 5, below, 0.0))
            else:
                up, down = (5, 3) if name == "r" else (3, 5)
                beyond = jnp.where(row < 2, pltpu.roll(above, up, 0), jnp.where(row >= 6, pltpu.roll(below, down, 0), 0.0))
        return jnp.concatenate([main, beyond], axis=0)

    def north(v):
        return pltpu.roll(v, 383, 1)

    def south(v):
        return pltpu.roll(v, 1, 1)

    def east(v):
        return pltpu.roll(v, 39, 0)

    def west(v):
        return pltpu.roll(v, 1, 0)

    k = [whole("k", j) for j in range(NK)]
    face_l = [4.0 * harmonic(k[j], k[j + 1]) for j in range(NR)]
    face_e = [harmonic(k[j], east(k[j])) for j in range(NR)]
    face_n = [harmonic(k[j], north(k[j])) for j in range(NR)]
    diag, z = [], []
    for j in range(NR):
        d = whole("s", j) + face_l[j] + face_e[j] + west(face_e[j]) + face_n[j] + south(face_n[j])
        if j:
            d = d + face_l[j - 1]
        d = jnp.where(d > 0.0, d, 1.0)
        diag.append(d)
        z.append(whole("r", j) / d)

    def apply(v, count):
        out = []
        for j in range(count):
            beside = face_l[j] * v[j + 1] + face_e[j] * east(v[j]) + west(face_e[j] * v[j])
            beside = beside + face_n[j] * north(v[j]) + south(face_n[j] * v[j])
            if j:
                beside = beside + face_l[j - 1] * v[j - 1]
            out.append(diag[j] * v[j] - beside)
        return out

    q = apply(z, 5)
    w = [q[j] / diag[j] for j in range(5)]
    u = apply(w, 4)
    totals = [jnp.zeros((8, 128), F32)] * 4
    for j in range(4):
        own = [v[j][:32, :256] for v in (z, q, w, u)]
        for ref, v in zip((z_ref, q_ref, w_ref, u_ref), own):
            ref[j] = v
        zo, qo, wo, uo = own
        rz = wide_ref[slab_index("r", j), :, :256] * zo
        for i, product in enumerate((rz, zo * qo, qo * wo, wo * uo)):
            for a in range(4):
                for b in range(2):
                    totals[i] = totals[i] + product[8 * a : 8 * a + 8, 128 * b : 128 * b + 128]
    lane = lax.broadcasted_iota(jnp.int32, (1, 128), 1)
    line = jnp.zeros((1, 128), F32)
    for i in range(4):
        line = jnp.where(lane == i, jnp.sum(totals[i]), line)
    for i in range(sums_ref.shape[0]):
        sums_ref[i] = line


def finish(sums_ref, r_ref, z_ref, q_ref, w_ref, u_ref, pressure_ref, residual_ref):
    core = lax.axis_index("c")
    line = sums_ref[0]
    for i in range(1, sums_ref.shape[0]):
        line = line + sums_ref[i]
    lane = lax.broadcasted_iota(jnp.int32, (1, 128), 1)
    rz, zq, qw, wu = (jnp.sum(jnp.where(lane == i, line, 0.0), axis=1, keepdims=True) for i in range(4))
    alpha = rz / zq
    rz_next = alpha * alpha * qw - rz
    grown = 1.0 + rz_next / rz
    curve = grown * grown * zq - 2.0 * grown * alpha * qw + alpha * alpha * wu
    alpha_next = rz_next / curve
    along = alpha + alpha_next * grown
    across = alpha * alpha_next
    for j in range(4):
        to = jnp.where(core == 0, j, 3 - j)
        pressure_ref[to] = along * z_ref[j] - across * w_ref[j]
        residual_ref[to] = r_ref[4 + j] - along * q_ref[j] + across * u_ref[j]


def call(kernel, *shapes, space=pltpu.VMEM, scratch=(), limit=32 * 1024 * 1024):
    def run(*args):
        return pl.pallas_call(
            kernel,
            out_shape=[jax.ShapeDtypeStruct(shape, F32) for shape in shapes],
            in_specs=[pl.BlockSpec(memory_space=space)] * len(args),
            out_specs=[pl.BlockSpec(memory_space=pltpu.VMEM)] * len(shapes),
            scratch_shapes=scratch,
            compiler_params=pltpu.CompilerParams(vmem_limit_bytes=limit),
        )(*args)

    return run


def chain(count):
    up = [(i, i + 1) for i in range(count - 1)]
    return up, [(target, source) for source, target in up]


def groups(size, axes):
    ids = np.arange(math.prod(size.values())).reshape([size[axis] for axis in ALL])
    for i, first in enumerate((3 * size["z"] // 4, size["y"] // 2, size["x"] // 2, size["c"] // 2)):
        ids = np.roll(ids, -first, i)
    own = [ALL.index(axis) for axis in axes]
    rest = [i for i in range(len(ALL)) if i not in own]
    return ids.transpose(rest + own).reshape(-1, math.prod(size[axis] for axis in axes)).tolist()


def per_device(recharge, conductivity, storage):
    size = {axis: lax.axis_size(axis) for axis in ALL}
    block = (4, 32, 256)
    scratch = [pltpu.VMEM(block, F32)] * 3 + [pltpu.SemaphoreType.DMA((3,))]
    near = size["x"] * size["c"]
    own, out, side = call(
        pack_own, (12, 32, 256), (7, 32, 256), (near, 32, 128), space=pltpu.HBM, scratch=scratch
    )(*(pltpu.with_memory_space_constraint(v, pltpu.HBM) for v in (recharge, conductivity, storage)))
    beside = lax.ppermute(out, "c", [(0, 1), (1, 0)])
    side = lax.all_to_all(side, ("x", "c"), 0, 0)
    pack = functools.partial(pack_east, size["x"])
    wide, low, high = call(pack, (SLABS, 32, 384), (6, 8, 384), (6, 8, 384))(own, beside, side)
    up, down = chain(size["z"] * size["y"])
    from_low, from_high = lax.ppermute(high, EAST, up), lax.ppermute(low, EAST, down)
    z, q, w, u, sums = call(operate, block, block, block, block, (size["z"] * size["c"], 1, 128))(wide, from_low, from_high)
    sums = lax.all_to_all(sums, ALL, 0, 0, axis_index_groups=groups(size, ("z", "c")))
    line = jnp.sum(sums, axis=0)
    sums = jnp.broadcast_to(line[None], (size["y"] * size["x"], 1, 128))
    sums = lax.all_to_all(sums, ALL, 0, 0, axis_index_groups=groups(size, ("y", "x")))
    return tuple(call(finish, block, block)(sums, own, z, q, w, u))


def solution(mesh):
    east, north, layer = (mesh.shape[axis] for axis in ("east", "north", "layer"))
    row = 8 if east % 8 == 0 else 1
    fine = Mesh(mesh.devices.reshape(east // row, row, north, layer), ALL)
    placed = P("c", EAST, "x")
    return jax.shard_map(
        per_device, mesh=fine, in_specs=(placed,) * 3, out_specs=(placed,) * 2, check_vma=False
    )
```

```python
import functools
import math

import jax
import jax.numpy as jnp
import numpy as np
from jax import lax
from jax.experimental import pallas as pl
from jax.experimental.pallas import tpu as pltpu
from jax.sharding import Mesh, PartitionSpec as P

EAST = ("z", "y")
ALL = ("z", "y", "x", "c")
F32 = jnp.float32

NK, NR = 7, 6
SIDE = [("k", j) for j in range(6)] + [("r", j) for j in range(5)] + [("s", j) for j in range(5)]
OWN = {"k": 0, "r": 4, "s": 8}
HALF = 64


def sends_low_first():
    return lax.rem(lax.axis_index("y"), 2) == 0


def pack_own(r_hbm, k_hbm, s_hbm, own_ref, first_ref, second_ref, r_ref, k_ref, s_ref, arrived):
    copies = [
        pltpu.make_async_copy(source, target, arrived.at[i])
        for i, (source, target) in enumerate(((k_hbm, k_ref), (r_hbm, r_ref), (s_hbm, s_ref)))
    ]
    for copy in copies:
        copy.start()
    core, flip = lax.axis_index("c"), sends_low_first()
    row = lax.broadcasted_iota(jnp.int32, (8, 256), 0)
    for copy, ref, name in zip(copies, (k_ref, r_ref, s_ref), "krs"):
        copy.wait()
        for j in range(4):
            own_ref[OWN[name] + j] = ref[jnp.where(core == 0, j, 3 - j)]
    for j in range(4):
        k, r, s = (own_ref[OWN[name] + j] for name in "krs")
        low = jnp.where(row < 3, k[:8], jnp.where(row < 5, pltpu.roll(r[:8], 3, 0), pltpu.roll(s[:8], 5, 0)))
        high = jnp.where(row >= 5, k[24:], jnp.where(row >= 3, pltpu.roll(r[24:], 5, 0), pltpu.roll(s[24:], 3, 0)))
        first_ref[j] = jnp.where(flip, low, high)
        second_ref[j] = jnp.where(flip, high, low)


def widen(own_ref, first_ref, second_ref, tall_ref, out_ref, side_ref):
    flip = sends_low_first()
    row = lax.broadcasted_iota(jnp.int32, (8, 256), 0)
    lane = lax.broadcasted_iota(jnp.int32, (40, 128), 1)
    line = jnp.zeros((40, 128), F32)
    at = 0
    for name, count in (("k", 3), ("r", 2), ("s", 2)):
        slabs = []
        for j in range(4):
            below = jnp.where(flip, first_ref[j], second_ref[j])
            above = jnp.where(flip, second_ref[j], first_ref[j])
            if name == "k":
                beyond = jnp.where(row < 3, above, jnp.where(row >= 5, below, 0.0))
            else:
                up, down = (5, 3) if name == "r" else (3, 5)
                beyond = jnp.where(row < 2, pltpu.roll(above, up, 0), jnp.where(row >= 6, pltpu.roll(below, down, 0), 0.0))
            i = OWN[name] + j
            slab = jnp.concatenate([own_ref[i], beyond], axis=0)
            tall_ref[i] = slab
            slabs.append(slab)
            low, high = slab[:, :128], pltpu.roll(slab[:, 128:], 3 * i + HALF + 3, 1)
            low = pltpu.roll(low, 3 * i, 1) if i else low
            line = jnp.where((lane >= 3 * i) & (lane < 3 * i + 3), low, line)
            line = jnp.where((lane >= HALF + 3 * i) & (lane < HALF + 3 * i + 3), high, line)
        for j in range(count):
            out_ref[at] = slabs[3 - j]
            at += 1
    for i in range(side_ref.shape[0]):
        side_ref[i] = line


def harmonic(first, second):
    return 2.0 * first * second / jnp.maximum(first + second, 1e-30)


def operate(north_count, tall_ref, in_ref, side_ref, z_ref, q_ref, w_ref, u_ref, sums_ref):
    lane = lax.broadcasted_iota(jnp.int32, (40, 128), 1)
    core, place = lax.axis_index("c"), lax.axis_index("x")
    up, down = jnp.minimum(place + 1, north_count - 1), jnp.maximum(place - 1, 0)
    has_up, has_down = place < north_count - 1, place > 0
    same = (side_ref[2 * up + core], side_ref[2 * down + core])
    other = (side_ref[2 * up + 1 - core], side_ref[2 * down + 1 - core])
    take_up, take_down = (lane < 3) & has_up, (lane >= 125) & has_down

    def whole(name, j):
        main = tall_ref[OWN[name] + j] if j < 4 else in_ref[{"k": 0, "r": 3, "s": 5}[name] + j - 4]
        beyond = jnp.zeros((40, 128), F32)
        if (name, j) in SIDE:
            above, below = same if j < 4 else other
            i = OWN[name] + (j if j < 4 else 7 - j)
            above = pltpu.roll(above, 128 - 3 * i, 1) if i else above
            below = pltpu.roll(below, (125 - HALF - 3 * i) % 128, 1)
            beyond = jnp.where(take_up, above, jnp.where(take_down, below, 0.0))
        return jnp.concatenate([main, beyond], axis=1)

    def north(v):
        return pltpu.roll(v, 383, 1)

    def south(v):
        return pltpu.roll(v, 1, 1)

    def east(v):
        return pltpu.roll(v, 39, 0)

    def west(v):
        return pltpu.roll(v, 1, 0)

    k = [whole("k", j) for j in range(NK)]
    face_l = [4.0 * harmonic(k[j], k[j + 1]) for j in range(NR)]
    face_e = [harmonic(k[j], east(k[j])) for j in range(NR)]
    face_n = [harmonic(k[j], north(k[j])) for j in range(NR)]
    diag, z = [], []
    for j in range(NR):
        d = whole("s", j) + face_l[j] + face_e[j] + west(face_e[j]) + face_n[j] + south(face_n[j])
        if j:
            d = d + face_l[j - 1]
        d = jnp.where(d > 0.0, d, 1.0)
        diag.append(d)
        z.append(whole("r", j) / d)

    def apply(v, count):
        out = []
        for j in range(count):
            beside = face_l[j] * v[j + 1] + face_e[j] * east(v[j]) + west(face_e[j] * v[j])
            beside = beside + face_n[j] * north(v[j]) + south(face_n[j] * v[j])
            if j:
                beside = beside + face_l[j - 1] * v[j - 1]
            out.append(diag[j] * v[j] - beside)
        return out

    q = apply(z, 5)
    w = [q[j] / diag[j] for j in range(5)]
    u = apply(w, 4)
    totals = [jnp.zeros((8, 128), F32)] * 4
    for j in range(4):
        own = [v[j][:32, :256] for v in (z, q, w, u)]
        for ref, v in zip((z_ref, q_ref, w_ref, u_ref), own):
            ref[j] = v
        zo, qo, wo, uo = own
        rz = tall_ref[OWN["r"] + j, :32, :] * zo
        for i, product in enumerate((rz, zo * qo, qo * wo, wo * uo)):
            for a in range(4):
                for b in range(2):
                    totals[i] = totals[i] + product[8 * a : 8 * a + 8, 128 * b : 128 * b + 128]
    lane = lax.broadcasted_iota(jnp.int32, (1, 128), 1)
    line = jnp.zeros((1, 128), F32)
    for i in range(4):
        line = jnp.where(lane == i, jnp.sum(totals[i]), line)
    for i in range(sums_ref.shape[0]):
        sums_ref[i] = line


def finish(sums_ref, r_ref, z_ref, q_ref, w_ref, u_ref, pressure_ref, residual_ref):
    core = lax.axis_index("c")
    line = sums_ref[0]
    for i in range(1, sums_ref.shape[0]):
        line = line + sums_ref[i]
    lane = lax.broadcasted_iota(jnp.int32, (1, 128), 1)
    rz, zq, qw, wu = (jnp.sum(jnp.where(lane == i, line, 0.0), axis=1, keepdims=True) for i in range(4))
    alpha = rz / zq
    rz_next = alpha * alpha * qw - rz
    grown = 1.0 + rz_next / rz
    curve = grown * grown * zq - 2.0 * grown * alpha * qw + alpha * alpha * wu
    alpha_next = rz_next / curve
    along = alpha + alpha_next * grown
    across = alpha * alpha_next
    for j in range(4):
        to = jnp.where(core == 0, j, 3 - j)
        pressure_ref[to] = along * z_ref[j] - across * w_ref[j]
        residual_ref[to] = r_ref[4 + j] - along * q_ref[j] + across * u_ref[j]


def call(kernel, *shapes, space=pltpu.VMEM, scratch=(), limit=32 * 1024 * 1024):
    def run(*args):
        return pl.pallas_call(
            kernel,
            out_shape=[jax.ShapeDtypeStruct(shape, F32) for shape in shapes],
            in_specs=[pl.BlockSpec(memory_space=space)] * len(args),
            out_specs=[pl.BlockSpec(memory_space=pltpu.VMEM)] * len(shapes),
            scratch_shapes=scratch,
            compiler_params=pltpu.CompilerParams(vmem_limit_bytes=limit),
        )(*args)

    return run


def pairs(count, start):
    up = [(i, i + 1) for i in range(start, count - 1, 2)]
    return up + [(target, source) for source, target in up]


def groups(size, axes):
    ids = np.arange(math.prod(size.values())).reshape([size[axis] for axis in ALL])
    for i, first in enumerate((3 * size["z"] // 4, size["y"] // 2, size["x"] // 2, size["c"] // 2)):
        ids = np.roll(ids, -first, i)
    own = [ALL.index(axis) for axis in axes]
    rest = [i for i in range(len(ALL)) if i not in own]
    return ids.transpose(rest + own).reshape(-1, math.prod(size[axis] for axis in axes)).tolist()


def per_device(recharge, conductivity, storage):
    size = {axis: lax.axis_size(axis) for axis in ALL}
    block = (4, 32, 256)
    scratch = [pltpu.VMEM(block, F32)] * 3 + [pltpu.SemaphoreType.DMA((3,))]
    near = size["x"] * size["c"]
    own, first, second = call(
        pack_own, (12, 32, 256), (4, 8, 256), (4, 8, 256), space=pltpu.HBM, scratch=scratch
    )(*(pltpu.with_memory_space_constraint(v, pltpu.HBM) for v in (recharge, conductivity, storage)))
    odd, even = pairs(size["z"] * size["y"], 1), pairs(size["z"] * size["y"], 0)
    first, second = lax.ppermute(first, EAST, odd), lax.ppermute(second, EAST, even)
    tall, out, side = call(widen, (12, 40, 256), (7, 40, 256), (near, 40, 128))(own, first, second)
    beside = lax.ppermute(out, "c", [(0, 1), (1, 0)])
    side = lax.all_to_all(side, ("x", "c"), 0, 0)
    apply_both = functools.partial(operate, size["x"])
    z, q, w, u, sums = call(apply_both, block, block, block, block, (size["z"] * size["c"], 1, 128))(tall, beside, side)
    sums = lax.all_to_all(sums, ALL, 0, 0, axis_index_groups=groups(size, ("z", "c")))
    line = jnp.sum(sums, axis=0)
    sums = jnp.broadcast_to(line[None], (size["y"] * size["x"], 1, 128))
    sums = lax.all_to_all(sums, ALL, 0, 0, axis_index_groups=groups(size, ("y", "x")))
    return tuple(call(finish, block, block)(sums, own, z, q, w, u))


def solution(mesh):
    east, north, layer = (mesh.shape[axis] for axis in ("east", "north", "layer"))
    row = 8 if east % 8 == 0 else 1
    fine = Mesh(mesh.devices.reshape(east // row, row, north, layer), ALL)
    placed = P("c", EAST, "x")
    return jax.shard_map(
        per_device, mesh=fine, in_specs=(placed,) * 3, out_specs=(placed,) * 2, check_vma=False
    )
```

```python
import functools
import math

import jax
import jax.numpy as jnp
import numpy as np
from jax import lax
from jax.experimental import pallas as pl
from jax.experimental.pallas import tpu as pltpu
from jax.sharding import Mesh, PartitionSpec as P

EAST = ("z", "y")
ALL = ("z", "y", "x", "c")
F32 = jnp.float32

NK, NR = 7, 6
SIDE = [("k", j) for j in range(6)] + [("r", j) for j in range(5)] + [("s", j) for j in range(5)]
OWN = {"k": 0, "r": 4, "s": 8}
WIDTH = {"k": 3, "r": 2, "s": 2}
HALF = 32


def first_lane(name, j):
    return {"k": 0, "r": 12, "s": 20}[name] + WIDTH[name] * j


def sends_low_first():
    return lax.rem(lax.axis_index("y"), 2) == 0


def pack_own(r_hbm, k_hbm, s_hbm, own_ref, first_ref, second_ref, r_ref, k_ref, s_ref, arrived):
    copies = [
        pltpu.make_async_copy(source, target, arrived.at[i])
        for i, (source, target) in enumerate(((k_hbm, k_ref), (r_hbm, r_ref), (s_hbm, s_ref)))
    ]
    for copy in copies:
        copy.start()
    core, flip = lax.axis_index("c"), sends_low_first()
    row = lax.broadcasted_iota(jnp.int32, (8, 256), 0)
    for copy, ref, name in zip(copies, (k_ref, r_ref, s_ref), "krs"):
        copy.wait()
        for j in range(4):
            own_ref[OWN[name] + j] = ref[jnp.where(core == 0, j, 3 - j)]
    for j in range(4):
        k, r, s = (own_ref[OWN[name] + j] for name in "krs")
        low = jnp.where(row < 3, k[:8], jnp.where(row < 5, pltpu.roll(r[:8], 3, 0), pltpu.roll(s[:8], 5, 0)))
        high = jnp.where(row >= 5, k[24:], jnp.where(row >= 3, pltpu.roll(r[24:], 5, 0), pltpu.roll(s[24:], 3, 0)))
        first_ref[j] = jnp.where(flip, low, high)
        second_ref[j] = jnp.where(flip, high, low)


def pack_layer(own_ref, out_ref):
    at = 0
    for name, count in (("k", 3), ("r", 2), ("s", 2)):
        for j in range(count):
            out_ref[at] = own_ref[OWN[name] + 3 - j]
            at += 1


def widen(own_ref, first_ref, second_ref, tall_ref, side_ref):
    flip = sends_low_first()
    row = lax.broadcasted_iota(jnp.int32, (8, 256), 0)
    lane = lax.broadcasted_iota(jnp.int32, (40, 128), 1)
    line = jnp.zeros((40, 128), F32)
    rows = {}
    for name in "krs":
        for j in range(4):
            below = jnp.where(flip, first_ref[j], second_ref[j])
            above = jnp.where(flip, second_ref[j], first_ref[j])
            if name == "k":
                beyond = jnp.where(row < 3, above, jnp.where(row >= 5, below, 0.0))
            else:
                up, down = (5, 3) if name == "r" else (3, 5)
                beyond = jnp.where(row < 2, pltpu.roll(above, up, 0), jnp.where(row >= 6, pltpu.roll(below, down, 0), 0.0))
            rows[name, j] = beyond
            i = OWN[name] + j
            slab = jnp.concatenate([own_ref[i], beyond], axis=0)
            tall_ref[i] = slab
            at, width = first_lane(name, j), WIDTH[name]
            low, high = slab[:, :128], pltpu.roll(slab[:, 128:], at + HALF + width, 1)
            low = pltpu.roll(low, at, 1) if at else low
            line = jnp.where((lane >= at) & (lane < at + width), low, line)
            line = jnp.where((lane >= HALF + at) & (lane < HALF + at + width), high, line)
    folded = jnp.concatenate([pltpu.roll(line[24:], 64, 1), jnp.zeros((8, 128), F32)], axis=0)
    line = jnp.where(lane[:24] < 64, line[:24], folded)
    for i in range(side_ref.shape[0]):
        side_ref[i] = line
    mixed = rows["k", 3]
    for to, back, slab in ((2, 5, rows["k", 2]), (3, 4, rows["r", 3])):
        mixed = jnp.where(row == to, pltpu.roll(slab, to, 0), mixed)
        mixed = jnp.where(row == back, pltpu.roll(slab, back + 1, 0), mixed)
    last, narrow = rows["s", 3], row[:, :128]
    right = jnp.where(narrow == 1, pltpu.roll(last[:, 128:], 1, 0), pltpu.roll(last[:, 128:], 7, 0))
    last = jnp.where((narrow == 0) | (narrow == 7), last[:, :128], right)
    to = 2 * lax.axis_index("x") + 1 - lax.axis_index("c")
    for i, tile in enumerate((mixed[:, :128], mixed[:, 128:], last)):
        side_ref[to, 8 * i : 8 * i + 8, :] = tile


def harmonic(first, second):
    return 2.0 * first * second / jnp.maximum(first + second, 1e-30)


def operate(north_count, tall_ref, in_ref, side_ref, z_ref, q_ref, w_ref, u_ref, sums_ref):
    lane = lax.broadcasted_iota(jnp.int32, (40, 128), 1)
    core, place = lax.axis_index("c"), lax.axis_index("x")
    up, down = jnp.minimum(place + 1, north_count - 1), jnp.maximum(place - 1, 0)
    has_up, has_down = place < north_count - 1, place > 0

    def line(at):
        folded = side_ref[at]
        return jnp.concatenate([folded, pltpu.roll(folded[:16], 64, 1)], axis=0)

    same = (line(2 * up + core), line(2 * down + core))
    other = (line(2 * up + 1 - core), line(2 * down + 1 - core))

    row = lax.broadcasted_iota(jnp.int32, (8, 256), 0)
    across = side_ref[2 * place + 1 - core]
    mixed, last, narrow = jnp.concatenate([across[:8], across[8:16]], axis=1), across[16:], row[:, :128]
    right = jnp.where(narrow == 0, pltpu.roll(last, 7, 0), pltpu.roll(last, 1, 0))
    spread = {
        ("k", 4): (mixed, mixed),
        ("k", 5): (pltpu.roll(mixed, 6, 0), pltpu.roll(mixed, 2, 0)),
        ("r", 4): (pltpu.roll(mixed, 5, 0), pltpu.roll(mixed, 3, 0)),
        ("s", 4): (jnp.concatenate([last, right], axis=1),) * 2,
    }

    def whole(name, j):
        if j < 4:
            main = tall_ref[OWN[name] + j]
        else:
            tile = jnp.zeros((8, 256), F32)
            if (name, j) in spread:
                deep = 2 if (name, j) == ("k", 4) else 1
                above, below = spread[name, j]
                tile = jnp.where(row < deep, above, jnp.where(row >= 8 - deep, below, 0.0))
            main = jnp.concatenate([in_ref[{"k": 0, "r": 3, "s": 5}[name] + j - 4], tile], axis=0)
        beyond = jnp.zeros((40, 128), F32)
        if (name, j) in SIDE:
            above, below = same if j < 4 else other
            at, width = first_lane(name, j if j < 4 else 7 - j), WIDTH[name]
            above = pltpu.roll(above, 128 - at, 1) if at else above
            below = pltpu.roll(below, 128 - HALF - width - at, 1)
            take_up, take_down = (lane < width) & has_up, (lane >= 128 - width) & has_down
            beyond = jnp.where(take_up, above, jnp.where(take_down, below, 0.0))
        return jnp.concatenate([main, beyond], axis=1)

    def north(v):
        return pltpu.roll(v, 383, 1)

    def south(v):
        return pltpu.roll(v, 1, 1)

    def east(v):
        return pltpu.roll(v, 39, 0)

    def west(v):
        return pltpu.roll(v, 1, 0)

    k = [whole("k", j) for j in range(NK)]
    face_l = [4.0 * harmonic(k[j], k[j + 1]) for j in range(NR)]
    face_e = [harmonic(k[j], east(k[j])) for j in range(NR)]
    face_n = [harmonic(k[j], north(k[j])) for j in range(NR)]
    diag, z = [], []
    for j in range(NR):
        d = whole("s", j) + face_l[j] + face_e[j] + west(face_e[j]) + face_n[j] + south(face_n[j])
        if j:
            d = d + face_l[j - 1]
        d = jnp.where(d > 0.0, d, 1.0)
        diag.append(d)
        z.append(whole("r", j) / d)

    def apply(v, count):
        out = []
        for j in range(count):
            beside = face_l[j] * v[j + 1] + face_e[j] * east(v[j]) + west(face_e[j] * v[j])
            beside = beside + face_n[j] * north(v[j]) + south(face_n[j] * v[j])
            if j:
                beside = beside + face_l[j - 1] * v[j - 1]
            out.append(diag[j] * v[j] - beside)
        return out

    q = apply(z, 5)
    w = [q[j] / diag[j] for j in range(5)]
    u = apply(w, 4)
    totals = [jnp.zeros((8, 128), F32)] * 4
    for j in range(4):
        own = [v[j][:32, :256] for v in (z, q, w, u)]
        for ref, v in zip((z_ref, q_ref, w_ref, u_ref), own):
            ref[j] = v
        zo, qo, wo, uo = own
        rz = tall_ref[OWN["r"] + j, :32, :] * zo
        for i, product in enumerate((rz, zo * qo, qo * wo, wo * uo)):
            for a in range(4):
                for b in range(2):
                    totals[i] = totals[i] + product[8 * a : 8 * a + 8, 128 * b : 128 * b + 128]
    lane = lax.broadcasted_iota(jnp.int32, (1, 128), 1)
    line = jnp.zeros((1, 128), F32)
    for i in range(4):
        line = jnp.where(lane == i, jnp.sum(totals[i]), line)
    for i in range(sums_ref.shape[0]):
        sums_ref[i] = line


def finish(sums_ref, r_ref, z_ref, q_ref, w_ref, u_ref, pressure_ref, residual_ref):
    core = lax.axis_index("c")
    line = sums_ref[0]
    for i in range(1, sums_ref.shape[0]):
        line = line + sums_ref[i]
    lane = lax.broadcasted_iota(jnp.int32, (1, 128), 1)
    rz, zq, qw, wu = (jnp.sum(jnp.where(lane == i, line, 0.0), axis=1, keepdims=True) for i in range(4))
    alpha = rz / zq
    rz_next = alpha * alpha * qw - rz
    grown = 1.0 + rz_next / rz
    curve = grown * grown * zq - 2.0 * grown * alpha * qw + alpha * alpha * wu
    alpha_next = rz_next / curve
    along = alpha + alpha_next * grown
    across = alpha * alpha_next
    for j in range(4):
        to = jnp.where(core == 0, j, 3 - j)
        pressure_ref[to] = along * z_ref[j] - across * w_ref[j]
        residual_ref[to] = r_ref[4 + j] - along * q_ref[j] + across * u_ref[j]


def call(kernel, *shapes, space=pltpu.VMEM, scratch=(), limit=32 * 1024 * 1024):
    def run(*args):
        return pl.pallas_call(
            kernel,
            out_shape=[jax.ShapeDtypeStruct(shape, F32) for shape in shapes],
            in_specs=[pl.BlockSpec(memory_space=space)] * len(args),
            out_specs=[pl.BlockSpec(memory_space=pltpu.VMEM)] * len(shapes),
            scratch_shapes=scratch,
            compiler_params=pltpu.CompilerParams(vmem_limit_bytes=limit),
        )(*args)

    return run


def pairs(count, start):
    up = [(i, i + 1) for i in range(start, count - 1, 2)]
    return up + [(target, source) for source, target in up]


def groups(size, axes):
    ids = np.arange(math.prod(size.values())).reshape([size[axis] for axis in ALL])
    for i, first in enumerate((3 * size["z"] // 4, size["y"] // 2, size["x"] // 2, size["c"] // 2)):
        ids = np.roll(ids, -first, i)
    own = [ALL.index(axis) for axis in axes]
    rest = [i for i in range(len(ALL)) if i not in own]
    return ids.transpose(rest + own).reshape(-1, math.prod(size[axis] for axis in axes)).tolist()


def per_device(recharge, conductivity, storage):
    size = {axis: lax.axis_size(axis) for axis in ALL}
    block = (4, 32, 256)
    scratch = [pltpu.VMEM(block, F32)] * 3 + [pltpu.SemaphoreType.DMA((3,))]
    near = size["x"] * size["c"]
    own, first, second = call(
        pack_own, (12, 32, 256), (4, 8, 256), (4, 8, 256), space=pltpu.HBM, scratch=scratch
    )(*(pltpu.with_memory_space_constraint(v, pltpu.HBM) for v in (recharge, conductivity, storage)))
    odd, even = pairs(size["z"] * size["y"], 1), pairs(size["z"] * size["y"], 0)
    first, second = lax.ppermute(first, EAST, odd), lax.ppermute(second, EAST, even)
    (out,) = call(pack_layer, (7, 32, 256))(own)
    beside = lax.ppermute(out, "c", [(0, 1), (1, 0)])
    tall, side = call(widen, (12, 40, 256), (near, 24, 128))(own, first, second)
    side = lax.all_to_all(side, ("x", "c"), 0, 0)
    apply_both = functools.partial(operate, size["x"])
    z, q, w, u, sums = call(apply_both, block, block, block, block, (size["z"] * size["c"], 1, 128))(tall, beside, side)
    sums = lax.all_to_all(sums, ALL, 0, 0, axis_index_groups=groups(size, ("z", "c")))
    line = jnp.sum(sums, axis=0)
    sums = jnp.broadcast_to(line[None], (size["y"] * size["x"], 1, 128))
    sums = lax.all_to_all(sums, ALL, 0, 0, axis_index_groups=groups(size, ("y", "x")))
    return tuple(call(finish, block, block)(sums, own, z, q, w, u))


def solution(mesh):
    east, north, layer = (mesh.shape[axis] for axis in ("east", "north", "layer"))
    row = 8 if east % 8 == 0 else 1
    fine = Mesh(mesh.devices.reshape(east // row, row, north, layer), ALL)
    placed = P("c", EAST, "x")
    return jax.shard_map(
        per_device, mesh=fine, in_specs=(placed,) * 3, out_specs=(placed,) * 2, check_vma=False
    )
```

```python
import functools
import math

import jax
import jax.numpy as jnp
import numpy as np
from jax import lax
from jax.experimental import pallas as pl
from jax.experimental.pallas import tpu as pltpu
from jax.sharding import Mesh, PartitionSpec as P

EAST = ("z", "y")
ALL = ("z", "y", "x", "c")
F32 = jnp.float32

NK, NR = 7, 6
SIDE = [("k", j) for j in range(6)] + [("r", j) for j in range(5)] + [("s", j) for j in range(5)]
OWN = {"k": 0, "r": 4, "s": 8}
WIDTH = {"k": 3, "r": 2, "s": 2}
HALF = 32


def first_lane(name, j):
    return {"k": 0, "r": 12, "s": 20}[name] + WIDTH[name] * j


def sends_low_first():
    return lax.rem(lax.axis_index("y"), 2) == 0


def pack_own(r_hbm, k_hbm, s_hbm, own_ref, first_ref, second_ref, r_ref, k_ref, s_ref, arrived):
    copies = [
        pltpu.make_async_copy(source, target, arrived.at[i])
        for i, (source, target) in enumerate(((k_hbm, k_ref), (r_hbm, r_ref), (s_hbm, s_ref)))
    ]
    for copy in copies:
        copy.start()
    core, flip = lax.axis_index("c"), sends_low_first()
    row = lax.broadcasted_iota(jnp.int32, (8, 256), 0)
    for copy, ref, name in zip(copies, (k_ref, r_ref, s_ref), "krs"):
        copy.wait()
        for j in range(4):
            own_ref[OWN[name] + j] = ref[jnp.where(core == 0, j, 3 - j)]
    for j in range(4):
        k, r, s = (own_ref[OWN[name] + j] for name in "krs")
        low = jnp.where(row < 3, k[:8], jnp.where(row < 5, pltpu.roll(r[:8], 3, 0), pltpu.roll(s[:8], 5, 0)))
        high = jnp.where(row >= 5, k[24:], jnp.where(row >= 3, pltpu.roll(r[24:], 5, 0), pltpu.roll(s[24:], 3, 0)))
        first_ref[j] = jnp.where(flip, low, high)
        second_ref[j] = jnp.where(flip, high, low)


def pack_layer(own_ref, out_ref):
    at = 0
    for name, count in (("k", 3), ("r", 2), ("s", 2)):
        for j in range(count):
            out_ref[at] = own_ref[OWN[name] + 3 - j]
            at += 1


def widen(own_ref, first_ref, second_ref, tall_ref, side_ref):
    flip = sends_low_first()
    row = lax.broadcasted_iota(jnp.int32, (8, 256), 0)
    lane = lax.broadcasted_iota(jnp.int32, (40, 128), 1)
    line = jnp.zeros((40, 128), F32)
    rows = {}
    for name in "krs":
        for j in range(4):
            below = jnp.where(flip, first_ref[j], second_ref[j])
            above = jnp.where(flip, second_ref[j], first_ref[j])
            if name == "k":
                beyond = jnp.where(row < 3, above, jnp.where(row >= 5, below, 0.0))
            else:
                up, down = (5, 3) if name == "r" else (3, 5)
                beyond = jnp.where(row < 2, pltpu.roll(above, up, 0), jnp.where(row >= 6, pltpu.roll(below, down, 0), 0.0))
            rows[name, j] = beyond
            i = OWN[name] + j
            slab = jnp.concatenate([own_ref[i], beyond], axis=0)
            tall_ref[i] = slab
            at, width = first_lane(name, j), WIDTH[name]
            low, high = slab[:, :128], pltpu.roll(slab[:, 128:], at + HALF + width, 1)
            low = pltpu.roll(low, at, 1) if at else low
            line = jnp.where((lane >= at) & (lane < at + width), low, line)
            line = jnp.where((lane >= HALF + at) & (lane < HALF + at + width), high, line)
    folded = jnp.concatenate([pltpu.roll(line[24:], 64, 1), jnp.zeros((8, 128), F32)], axis=0)
    line = jnp.where(lane[:24] < 64, line[:24], folded)
    for i in range(side_ref.shape[0]):
        side_ref[i] = line
    mixed = rows["k", 3]
    for to, back, slab in ((2, 5, rows["k", 2]), (3, 4, rows["r", 3])):
        mixed = jnp.where(row == to, pltpu.roll(slab, to, 0), mixed)
        mixed = jnp.where(row == back, pltpu.roll(slab, back + 1, 0), mixed)
    last, narrow = rows["s", 3], row[:, :128]
    right = jnp.where(narrow == 1, pltpu.roll(last[:, 128:], 1, 0), pltpu.roll(last[:, 128:], 7, 0))
    last = jnp.where((narrow == 0) | (narrow == 7), last[:, :128], right)
    to = near_place(lax.axis_index("x"), side_ref.shape[0] // 2) + lax.axis_index("c")
    for i, tile in enumerate((mixed[:, :128], mixed[:, 128:], last)):
        side_ref[to, 8 * i : 8 * i + 8, :] = tile


def harmonic(first, second):
    return 2.0 * first * second / jnp.maximum(first + second, 1e-30)


def operate(north_count, tall_ref, in_ref, side_ref, z_ref, q_ref, w_ref, u_ref, sums_ref):
    lane = lax.broadcasted_iota(jnp.int32, (40, 128), 1)
    core, place = lax.axis_index("c"), lax.axis_index("x")
    up, down = jnp.minimum(place + 1, north_count - 1), jnp.maximum(place - 1, 0)
    up, down = near_place(up, north_count), near_place(down, north_count)
    has_up, has_down = place < north_count - 1, place > 0

    def line(at):
        folded = side_ref[at]
        return jnp.concatenate([folded, pltpu.roll(folded[:16], 64, 1)], axis=0)

    same = (line(up + 1 - core), line(down + 1 - core))
    other = (line(up + core), line(down + core))

    row = lax.broadcasted_iota(jnp.int32, (8, 256), 0)
    across = side_ref[near_place(place, north_count) + core]
    mixed, last, narrow = jnp.concatenate([across[:8], across[8:16]], axis=1), across[16:], row[:, :128]
    right = jnp.where(narrow == 0, pltpu.roll(last, 7, 0), pltpu.roll(last, 1, 0))
    spread = {
        ("k", 4): (mixed, mixed),
        ("k", 5): (pltpu.roll(mixed, 6, 0), pltpu.roll(mixed, 2, 0)),
        ("r", 4): (pltpu.roll(mixed, 5, 0), pltpu.roll(mixed, 3, 0)),
        ("s", 4): (jnp.concatenate([last, right], axis=1),) * 2,
    }

    def whole(name, j):
        if j < 4:
            main = tall_ref[OWN[name] + j]
        else:
            tile = jnp.zeros((8, 256), F32)
            if (name, j) in spread:
                deep = 2 if (name, j) == ("k", 4) else 1
                above, below = spread[name, j]
                tile = jnp.where(row < deep, above, jnp.where(row >= 8 - deep, below, 0.0))
            main = jnp.concatenate([in_ref[{"k": 0, "r": 3, "s": 5}[name] + j - 4], tile], axis=0)
        beyond = jnp.zeros((40, 128), F32)
        if (name, j) in SIDE:
            above, below = same if j < 4 else other
            at, width = first_lane(name, j if j < 4 else 7 - j), WIDTH[name]
            above = pltpu.roll(above, 128 - at, 1) if at else above
            below = pltpu.roll(below, 128 - HALF - width - at, 1)
            take_up, take_down = (lane < width) & has_up, (lane >= 128 - width) & has_down
            beyond = jnp.where(take_up, above, jnp.where(take_down, below, 0.0))
        return jnp.concatenate([main, beyond], axis=1)

    def north(v):
        return pltpu.roll(v, 383, 1)

    def south(v):
        return pltpu.roll(v, 1, 1)

    def east(v):
        return pltpu.roll(v, 39, 0)

    def west(v):
        return pltpu.roll(v, 1, 0)

    k = [whole("k", j) for j in range(NK)]
    face_l = [4.0 * harmonic(k[j], k[j + 1]) for j in range(NR)]
    face_e = [harmonic(k[j], east(k[j])) for j in range(NR)]
    face_n = [harmonic(k[j], north(k[j])) for j in range(NR)]
    diag, z = [], []
    for j in range(NR):
        d = whole("s", j) + face_l[j] + face_e[j] + west(face_e[j]) + face_n[j] + south(face_n[j])
        if j:
            d = d + face_l[j - 1]
        d = jnp.where(d > 0.0, d, 1.0)
        diag.append(d)
        z.append(whole("r", j) / d)

    def apply(v, count):
        out = []
        for j in range(count):
            beside = face_l[j] * v[j + 1] + face_e[j] * east(v[j]) + west(face_e[j] * v[j])
            beside = beside + face_n[j] * north(v[j]) + south(face_n[j] * v[j])
            if j:
                beside = beside + face_l[j - 1] * v[j - 1]
            out.append(diag[j] * v[j] - beside)
        return out

    q = apply(z, 5)
    w = [q[j] / diag[j] for j in range(5)]
    u = apply(w, 4)
    totals = [jnp.zeros((8, 128), F32)] * 4
    for j in range(4):
        own = [v[j][:32, :256] for v in (z, q, w, u)]
        for ref, v in zip((z_ref, q_ref, w_ref, u_ref), own):
            ref[j] = v
        zo, qo, wo, uo = own
        rz = tall_ref[OWN["r"] + j, :32, :] * zo
        for i, product in enumerate((rz, zo * qo, qo * wo, wo * uo)):
            for a in range(4):
                for b in range(2):
                    totals[i] = totals[i] + product[8 * a : 8 * a + 8, 128 * b : 128 * b + 128]
    lane = lax.broadcasted_iota(jnp.int32, (1, 128), 1)
    line = jnp.zeros((1, 128), F32)
    for i in range(4):
        line = jnp.where(lane == i, jnp.sum(totals[i]), line)
    for i in range(sums_ref.shape[0]):
        sums_ref[i] = line


def finish(sums_ref, r_ref, z_ref, q_ref, w_ref, u_ref, pressure_ref, residual_ref):
    core = lax.axis_index("c")
    line = sums_ref[0]
    for i in range(1, sums_ref.shape[0]):
        line = line + sums_ref[i]
    lane = lax.broadcasted_iota(jnp.int32, (1, 128), 1)
    rz, zq, qw, wu = (jnp.sum(jnp.where(lane == i, line, 0.0), axis=1, keepdims=True) for i in range(4))
    alpha = rz / zq
    rz_next = alpha * alpha * qw - rz
    grown = 1.0 + rz_next / rz
    curve = grown * grown * zq - 2.0 * grown * alpha * qw + alpha * alpha * wu
    alpha_next = rz_next / curve
    along = alpha + alpha_next * grown
    across = alpha * alpha_next
    for j in range(4):
        to = jnp.where(core == 0, j, 3 - j)
        pressure_ref[to] = along * z_ref[j] - across * w_ref[j]
        residual_ref[to] = r_ref[4 + j] - along * q_ref[j] + across * u_ref[j]


def call(kernel, *shapes, space=pltpu.VMEM, scratch=(), limit=32 * 1024 * 1024):
    def run(*args):
        return pl.pallas_call(
            kernel,
            out_shape=[jax.ShapeDtypeStruct(shape, F32) for shape in shapes],
            in_specs=[pl.BlockSpec(memory_space=space)] * len(args),
            out_specs=[pl.BlockSpec(memory_space=pltpu.VMEM)] * len(shapes),
            scratch_shapes=scratch,
            compiler_params=pltpu.CompilerParams(vmem_limit_bytes=limit),
        )(*args)

    return run


def pairs(count, start):
    up = [(i, i + 1) for i in range(start, count - 1, 2)]
    return up + [(target, source) for source, target in up]


def groups(size, axes):
    ids = np.arange(math.prod(size.values())).reshape([size[axis] for axis in ALL])
    for i, first in enumerate((3 * size["z"] // 4, size["y"] // 2, size["x"] // 2, size["c"] // 2)):
        ids = np.roll(ids, -first, i)
    own = [ALL.index(axis) for axis in axes]
    rest = [i for i in range(len(ALL)) if i not in own]
    return ids.transpose(rest + own).reshape(-1, math.prod(size[axis] for axis in axes)).tolist()


def near_groups(size):
    ids = np.arange(math.prod(size.values())).reshape(-1, size["x"], size["c"])
    return np.roll(ids, -(size["x"] // 2), 1)[:, :, ::-1].reshape(-1, size["x"] * size["c"]).tolist()


def near_place(place, count):
    return 2 * lax.rem(place + count - count // 2, count)


def per_device(recharge, conductivity, storage):
    size = {axis: lax.axis_size(axis) for axis in ALL}
    block = (4, 32, 256)
    scratch = [pltpu.VMEM(block, F32)] * 3 + [pltpu.SemaphoreType.DMA((3,))]
    near = size["x"] * size["c"]
    own, first, second = call(
        pack_own, (12, 32, 256), (4, 8, 256), (4, 8, 256), space=pltpu.HBM, scratch=scratch
    )(*(pltpu.with_memory_space_constraint(v, pltpu.HBM) for v in (recharge, conductivity, storage)))
    odd, even = pairs(size["z"] * size["y"], 1), pairs(size["z"] * size["y"], 0)
    first, second = lax.ppermute(first, EAST, odd), lax.ppermute(second, EAST, even)
    (out,) = call(pack_layer, (7, 32, 256))(own)
    beside = lax.ppermute(out, "c", [(0, 1), (1, 0)])
    tall, side = call(widen, (12, 40, 256), (near, 24, 128))(own, first, second)
    side = lax.all_to_all(side, ALL, 0, 0, axis_index_groups=near_groups(size))
    apply_both = functools.partial(operate, size["x"])
    z, q, w, u, sums = call(apply_both, block, block, block, block, (size["z"] * size["c"], 1, 128))(tall, beside, side)
    sums = lax.all_to_all(sums, ALL, 0, 0, axis_index_groups=groups(size, ("z", "c")))
    line = jnp.sum(sums, axis=0)
    sums = jnp.broadcast_to(line[None], (size["y"] * size["x"], 1, 128))
    sums = lax.all_to_all(sums, ALL, 0, 0, axis_index_groups=groups(size, ("y", "x")))
    return tuple(call(finish, block, block)(sums, own, z, q, w, u))


def solution(mesh):
    east, north, layer = (mesh.shape[axis] for axis in ("east", "north", "layer"))
    row = 8 if east % 8 == 0 else 1
    fine = Mesh(mesh.devices.reshape(east // row, row, north, layer), ALL)
    placed = P("c", EAST, "x")
    return jax.shard_map(
        per_device, mesh=fine, in_specs=(placed,) * 3, out_specs=(placed,) * 2, check_vma=False
    )
```
